256 devices in a mesh: dp: 4 (over z_hi, core), expert: 16 (over y, x), fsdp: 4 (over z_lo).
Axes of the slice: x: 4, y: 4, z: 8 (z_hi: 2, z_lo: 4; z = z_hi * 4 + z_lo), core: 2. Of those that a mesh axis runs over, the one named last changes fastest.
Arguments:
- grads: bfloat16 [4, 96, 768, 2048], P('dp', 'expert', 'fsdp')
- momentum: float32 [96, 768, 2048], P('expert', 'fsdp', 'dp'), may hold values from -6 to 6
Outputs:
- direction: bfloat16 [96, 768, 2048], P('expert', 'fsdp', 'dp')
- new_momentum: float32 [96, 768, 2048], P('expert', 'fsdp', 'dp')
The draws below stay inside these ranges and needn't reach their ends.
All inputs are finite; a program needn't handle non-finite values.
Results may differ from the reference program's by a relative error of at most 0.015.
Values may be sent and summed in bfloat16 or wider, within the bound.
A program may use at most 128 MiB of HBM per device.

```python
import math
import jax
import jax.numpy as jnp
from jax import lax

ROWS = 768
COLS = 2048
ITERS = 2
EXPERTS = 32
MATS = 96
N_DP = 4


def draw_grads(key, part):
    key = jax.random.fold_in(key, 11)
    keys = jax.random.split(key, 3)
    shape = (N_DP, MATS, ROWS, COLS)
    row_scale = jnp.exp(jax.random.uniform(keys[0], (1, MATS, ROWS, 1)) * math.log(10.0))
    col_scale = jnp.exp(jax.random.uniform(keys[1], (1, MATS, 1, COLS)) * math.log(10.0))
    col_pos = jnp.arange(COLS).astype(jnp.float32) / max(COLS - 1, 1)
    expert_pos = (jnp.arange(MATS) // 3).astype(jnp.float32) / max(EXPERTS - 1, 1)
    mat_scale = (3.0 ** expert_pos).reshape(1, MATS, 1, 1)
    col_trend = (3.0 ** col_pos).reshape(1, 1, 1, COLS)
    noise = jax.random.normal(keys[2], shape, jnp.float32)
    return (noise * row_scale * col_scale * col_trend * mat_scale).astype(jnp.bfloat16)


def block_scale(rng, extent, pieces, low, top_value):
    gain = 1.0
    for dim, parts in pieces:
        steps = jax.random.uniform(jax.random.fold_in(jax.random.fold_in(rng, 6), dim), (parts,), jnp.float32, low / len(pieces), top_value / len(pieces))
        gain = gain * jnp.repeat(jnp.exp(steps), extent[dim] // parts).reshape((-1,) + (1,) * (len(extent) - 1 - dim))
    return gain


def scatter_about(own_key, shape, scale, bound, cuts=(), dtype=jnp.bfloat16):
    values = scale * jax.random.normal(own_key, shape, jnp.float32)
    if cuts:
        values = values * block_scale(own_key, shape, cuts, -0.22, 0.18)
    return jnp.clip(values, -bound, bound).astype(dtype)


def setup_inputs(seed: int = 0) -> dict:
    key_of = jax.random.split(jax.random.key(seed), 3)
    return {
        "grads": draw_grads(jax.random.fold_in(key_of[2], 71), 0),
        "momentum": scatter_about(key_of[1], (MATS, ROWS, COLS), 1.0, 6.0, ((0, 16), (1, 4), (2, 4)), jnp.float32),
    }


COEF_A = 3.4445
COEF_B = -4.775
COEF_C = 2.0315
DECAY = 0.95

def orthogonalize(matrix):
    values = matrix.astype(jnp.float32)
    norm = jnp.sqrt(jnp.sum(values * values))
    current = (values / (norm + 1e-07)).astype(jnp.bfloat16)
    result = values
    for sweep in range(ITERS):
        cur_f = current.astype(jnp.float32)
        gram = jnp.einsum('brc,bsc->rs', cur_f, cur_f).astype(jnp.bfloat16)
        square = jnp.dot(gram, gram, preferred_element_type=jnp.float32)
        poly = (COEF_B * gram.astype(jnp.float32) + COEF_C * square).astype(jnp.bfloat16)
        result = COEF_A * cur_f + jnp.einsum('rs,bsc->brc', poly.astype(jnp.float32), cur_f)
        if sweep + 1 < ITERS:
            current = result.astype(jnp.bfloat16)
    return result

def reference(grads, momentum):
    summed = lax.optimization_barrier(jnp.sum(grads.astype(jnp.float32), axis=0))
    total_sq = jnp.sum(summed * summed)
    count = jnp.float32(MATS * ROWS * COLS)
    clip = jnp.minimum(jnp.float32(1.0), 1.0 / jnp.sqrt(total_sq / count + 1e-06))
    new_momentum = DECAY * momentum + clip * summed
    nesterov = (clip * summed + DECAY * new_momentum).astype(jnp.bfloat16)
    factor = 0.2 * math.sqrt(max(ROWS, COLS))

    def one_matrix(matrix):
        return (factor * orthogonalize(matrix[None])[0]).astype(jnp.bfloat16)
    direction = lax.map(one_matrix, nesterov)
    return (direction, new_momentum)
```

```python
import functools
import math

import jax
import jax.numpy as jnp
from jax import lax
from jax.experimental import pallas as pl
from jax.experimental.pallas import tpu as pltpu
from jax.sharding import PartitionSpec as P

ROWS = 768
COLS = 2048
MATS = 6
RB = 192
CB = 512
RING = 8
PLANE = 16
COUNT = 96 * ROWS * COLS
SUB = 4
CW = CB // SUB
KW = 2 * CW
OWNER = (0, 1, 2, 4, 5, 6)
ORDER = (0, 2, 4, 1, 3, 5)

COEF_A = 3.4445
COEF_B = -4.775
COEF_C = 2.0315
DECAY = 0.95
FACTOR = 0.2 * math.sqrt(max(ROWS, COLS))

f32 = jnp.float32
bf16 = jnp.bfloat16


def kernel(
    g_hbm, m_hbm, dir_hbm, nm_hbm,
    gown, grec, psend, prec, summed, mom, nest, x0, x1, y, g_part, g_recv, gram, poly, col_sq, plane_sq,
    own_sem, mom_sem, cs_sem, cr_sem, rs_sem, rr_sem, sq_send, sq_recv,
    ns_sem, xr_sem, xl_sem, gs_sem, gr_sem, ds_sem, dr_sem, dl_sem, nm_sem,
):
    dp = lax.axis_index("dp")
    expert = lax.axis_index("expert")
    zl = lax.axis_index("fsdp")
    zh = dp // 2
    core = lax.rem(dp, 2)
    z = zh * 4 + zl
    other = 1 - core

    def at(zz, cc):
        zz = lax.rem(zz, RING)
        return {"dp": (zz // 4) * 2 + cc, "fsdp": lax.rem(zz, 4)}

    def remote(src, dst, send, recv, device):
        return pltpu.make_async_remote_copy(
            src_ref=src, dst_ref=dst, send_sem=send, recv_sem=recv, device_id=device
        )

    def block(index):
        return pl.ds(pl.multiple_of(index * CB, CB), CB)

    far = (1 - zh) * 2
    near = zh * 2
    own = []
    for i in range(MATS):
        own.append(pltpu.make_async_copy(g_hbm.at[0, i, :, block(far + core)], gown.at[0, i], own_sem.at[i]))
    own.append(pltpu.make_async_copy(g_hbm.at[0, :, :, block(near + core)], gown.at[1], own_sem.at[MATS]))
    for copy in own:
        copy.start()
    load_mom = pltpu.make_async_copy(m_hbm, mom, mom_sem)
    load_mom.start()

    barrier = pltpu.get_barrier_semaphore()
    for step in range(1, RING):
        for cc in (core, other):
            pl.semaphore_signal(barrier, inc=1, device_id=at(z + step, cc))
    pl.semaphore_signal(barrier, inc=1, device_id=at(z, other))
    for step in range(1, PLANE):
        pl.semaphore_signal(barrier, inc=1, device_id={"expert": lax.rem(expert + step, PLANE)})
    pl.semaphore_wait(barrier, 2 * RING - 1 + PLANE - 1)

    swap = []
    for i in range(MATS):
        swap.append(remote(
            g_hbm.at[0, i, :, block(far + other)], grec.at[0, i], cs_sem.at[i], cr_sem.at[i], at(z, other)
        ))
    swap.append(remote(
        g_hbm.at[0, :, :, block(near + other)], grec.at[1], cs_sem.at[MATS], cr_sem.at[MATS], at(z, other)
    ))
    for copy in swap:
        copy.start()

    def each(rows, step, work, init=0):
        return lax.fori_loop(
            0, rows // step, lambda t, carry: work(pl.ds(pl.multiple_of(t * step, step), step), carry), init
        )

    across = []
    for i in range(MATS):
        own[i].wait()
        swap[i].wait_recv()

        def add_far(rows, carry):
            psend[i, rows, :] = (gown[0, i, rows, :].astype(f32) + grec[0, i, rows, :].astype(f32)).astype(bf16)
            return carry

        each(RB, 32, add_far)
        copy = remote(psend.at[i], prec.at[i], rs_sem.at[i], rr_sem.at[i], at(z + 4, core))
        copy.start()
        across.append(copy)
    own[MATS].wait()
    swap[MATS].wait_recv()
    for i in range(MATS):

        def add_near(rows, carry):
            summed[i, rows, :] = gown[1, i, rows, :].astype(f32) + grec[1, i, rows, :].astype(f32)
            return carry

        each(RB, 32, add_near)
    for copy in swap:
        copy.wait_send()

    total = jnp.zeros((32, 128), f32)
    for i in range(MATS):
        across[i].wait_recv()

        def add_across(rows, carry):
            s = summed[i, rows, :] + prec[i, rows, :].astype(f32)
            summed[i, rows, :] = s
            q = s * s
            return carry + ((q[:, 0:128] + q[:, 128:256]) + (q[:, 256:384] + q[:, 384:512]))

        total = each(RB, 32, add_across, total)
    total = (total[0:8] + total[8:16]) + (total[16:24] + total[24:32])

    mine = z * 2 + core
    col_sq[mine] = total
    for step in range(1, RING):
        for cc in (core, other):
            remote(col_sq.at[mine], col_sq.at[mine], sq_send.at[0], sq_recv.at[0], at(z + step, cc)).start()
    remote(col_sq.at[mine], col_sq.at[mine], sq_send.at[0], sq_recv.at[0], at(z, other)).start()
    all_col = remote(
        col_sq.at[pl.ds(0, 2 * RING - 1)], col_sq.at[pl.ds(0, 2 * RING - 1)], sq_send.at[0], sq_recv.at[0], at(z, other)
    )
    all_col.wait_recv()
    plane_sq[expert] = jnp.sum(col_sq[...], axis=0)
    for step in range(1, PLANE):
        remote(
            plane_sq.at[expert], plane_sq.at[expert], sq_send.at[1], sq_recv.at[1],
            {"expert": lax.rem(expert + step, PLANE)},
        ).start()
    all_plane = remote(
        plane_sq.at[pl.ds(0, PLANE - 1)], plane_sq.at[pl.ds(0, PLANE - 1)], sq_send.at[1], sq_recv.at[1], at(z, other)
    )
    for copy in across:
        copy.wait_send()
    load_mom.wait()
    all_plane.wait_recv()
    total_sq = jnp.sum(jnp.sum(plane_sq[...], axis=0), axis=(0, 1), keepdims=True)
    clip = jnp.minimum(f32(1.0), 1.0 / jnp.sqrt(total_sq / f32(COUNT) + 1e-06))

    row_at = pl.ds(pl.multiple_of(zl * RB, RB), RB)
    half_at = pl.ds(pl.multiple_of(zh * CW, CW), CW)
    store_nm = []
    for i in ORDER:

        def momentum_step(rows, carry):
            s = clip * summed[i, rows, :]
            m = DECAY * mom[i, rows, :] + s
            mom[i, rows, :] = m
            nest[i, rows, :] = (s + DECAY * m).astype(bf16)
            return carry

        each(RB, 32, momentum_step)

        @pl.when(z != OWNER[i])
        def _():
            for k in range(SUB):
                remote(
                    nest.at[i, :, pl.ds(k * CW, CW)], x0.at[k, row_at, half_at], ns_sem.at[i], xr_sem.at[k],
                    at(jnp.int32(OWNER[i]), core),
                ).start()

        @pl.when(z == OWNER[i])
        def _():
            for k in range(SUB):
                pltpu.make_async_copy(
                    nest.at[i, :, pl.ds(k * CW, CW)], x0.at[k, row_at, half_at], xl_sem.at[k]
                ).start()

        copy = pltpu.make_async_copy(mom.at[i], nm_hbm.at[i], nm_sem.at[i])
        copy.start()
        store_nm.append(copy)

    mat = z - z // 4
    is_owner = lax.rem(z, 4) != 3

    def nt_dot(a, b):
        return lax.dot_general(a, b, (((1,), (1,)), ((), ())), preferred_element_type=f32)

    def nn_dot(a, b):
        return lax.dot_general(a, b, (((1,), (0,)), ((), ())), preferred_element_type=f32)

    def add_gram(sweep, x, k):
        def rows_of(rows, carry):
            g_part[sweep, rows, :] = g_part[sweep, rows, :] + nt_dot(x[k, rows, :], x[k])
            return carry

        each(ROWS, 256, rows_of)

    def swap_gram(sweep):
        return remote(
            g_part.at[sweep], g_recv.at[sweep], gs_sem.at[sweep], gr_sem.at[sweep], at(z, other)
        )

    def make_poly():
        def rows_of(rows, carry):
            g = gram[rows, :]
            square = nn_dot(g, gram[...])
            poly[rows, :] = (COEF_B * g.astype(f32) + COEF_C * square).astype(bf16)
            return carry

        each(ROWS, 256, rows_of)

    @pl.when(is_owner)
    def _():
        def clear(rows, carry):
            g_part[0, rows, :] = jnp.zeros((32, ROWS), f32)
            g_part[1, rows, :] = jnp.zeros((32, ROWS), f32)
            return carry

        each(ROWS, 32, clear)
        for k in range(SUB):
            pltpu.make_async_copy(nest.at[0, :, pl.ds(0, CW)], x0.at[k, row_at, half_at], xl_sem.at[k]).wait()
            seven = x0.at[k, pl.ds(0, (RING - 1) * RB // 2), :]
            remote(seven, seven, xr_sem.at[k], xr_sem.at[k], at(z, other)).wait_recv()
            add_gram(0, x0, k)
        copy = swap_gram(0)
        copy.start()
        copy.wait()

        diag = jnp.zeros((128, 128), f32)
        eye = lax.broadcasted_iota(jnp.int32, (128, 128), 0) == lax.broadcasted_iota(jnp.int32, (128, 128), 1)
        for b in range(ROWS // 128):
            s = pl.ds(b * 128, 128)
            diag = diag + jnp.where(eye, g_part[0, s, s] + g_recv[0, s, s], 0.0)
        norm = jnp.sqrt(jnp.sum(diag, axis=(0, 1), keepdims=True))
        inv = 1.0 / (norm + 1e-07)

        def scale_gram(rows, carry):
            gram[rows, :] = (((g_part[0, rows, :] + g_recv[0, rows, :]) * inv) * inv).astype(bf16)
            return carry

        each(ROWS, 32, scale_gram)
        make_poly()
        for k in range(SUB):

            def apply_first(rows, carry):
                v = COEF_A * x0[k, rows, :].astype(f32) + nn_dot(poly[rows, :], x0[k])
                x1[k, rows, :] = (v * inv).astype(bf16)
                return carry

            each(ROWS, 256, apply_first)
            add_gram(1, x1, k)
        copy = swap_gram(1)
        copy.start()
        copy.wait()

        def round_gram(rows, carry):
            gram[rows, :] = (g_part[1, rows, :] + g_recv[1, rows, :]).astype(bf16)
            return carry

        each(ROWS, 32, round_gram)
        make_poly()
        for k in range(SUB):

            def apply_last(rows, carry):
                v = COEF_A * x1[k, rows, :].astype(f32) + nn_dot(poly[rows, :], x1[k])
                y[k, rows, :] = (FACTOR * v).astype(bf16)
                return carry

            each(ROWS, 256, apply_last)
            part = pl.ds(k * CW, CW)
            for step in range(1, RING):
                there = lax.rem(z + step, RING)
                rows = pl.ds(pl.multiple_of(lax.rem(there, 4) * RB, RB), RB)
                cols = pl.ds(pl.multiple_of((there // 4) * CW, CW), CW)
                remote(
                    y.at[k, rows, cols], dir_hbm.at[mat, :, part], ds_sem.at[k], dr_sem.at[mat], at(there, core)
                ).start()
            pltpu.make_async_copy(y.at[k, row_at, half_at], dir_hbm.at[mat, :, part], dl_sem.at[k]).start()

    for i in range(MATS):

        @pl.when(z != OWNER[i])
        def _():
            done = remote(nest.at[i], dir_hbm.at[i], ns_sem.at[i], dr_sem.at[i], at(z, other))
            done.wait_send()
            done.wait_recv()

    @pl.when(is_owner)
    def _():
        for k in range(SUB):
            seven = y.at[k, pl.ds(0, (RING - 1) * RB // 2), :]
            remote(seven, seven, ds_sem.at[k], dr_sem.at[0], at(z, other)).wait_send()
            pltpu.make_async_copy(y.at[k, row_at, half_at], dir_hbm.at[mat, :, pl.ds(k * CW, CW)], dl_sem.at[k]).wait()

    all_col.wait_send()
    all_plane.wait_send()
    for copy in store_nm:
        copy.wait()


def on_device(grads, momentum):
    vmem = pltpu.VMEM
    dma = pltpu.SemaphoreType.DMA
    return pl.pallas_call(
        kernel,
        out_shape=(
            jax.ShapeDtypeStruct((MATS, RB, CB), bf16),
            jax.ShapeDtypeStruct((MATS, RB, CB), f32),
        ),
        in_specs=[pl.BlockSpec(memory_space=pl.ANY)] * 2,
        out_specs=(pl.BlockSpec(memory_space=pl.ANY),) * 2,
        scratch_shapes=[
            vmem((2, MATS, RB, CB), bf16),
            vmem((2, MATS, RB, CB), bf16),
            vmem((MATS, RB, CB), bf16),
            vmem((MATS, RB, CB), bf16),
            vmem((MATS, RB, CB), f32),
            vmem((MATS, RB, CB), f32),
            vmem((MATS, RB, CB), bf16),
            vmem((SUB, ROWS, KW), bf16),
            vmem((SUB, ROWS, KW), bf16),
            vmem((SUB, ROWS, KW), bf16),
            vmem((2, ROWS, ROWS), f32),
            vmem((2, ROWS, ROWS), f32),
            vmem((ROWS, ROWS), bf16),
            vmem((ROWS, ROWS), bf16),
            vmem((2 * RING, 8, 128), f32),
            vmem((PLANE, 8, 128), f32),
            dma((MATS + 1,)),
            dma,
            dma((MATS + 1,)),
            dma((MATS + 1,)),
            dma((MATS,)),
            dma((MATS,)),
            dma((2,)),
            dma((2,)),
            dma((MATS,)),
            dma((SUB,)),
            dma((SUB,)),
            dma((2,)),
            dma((2,)),
            dma((SUB,)),
            dma((MATS,)),
            dma((SUB,)),
            dma((MATS,)),
        ],
        compiler_params=pltpu.CompilerParams(
            collective_id=0, has_side_effects=True, vmem_limit_bytes=56 * 2**20
        ),
        cost_estimate=pl.CostEstimate(flops=7 * 10**9, bytes_accessed=12 * 10**6, transcendentals=0),
    )(grads, momentum)


def solution(mesh):
    in_specs = (P("dp", "expert", "fsdp", None), P("expert", "fsdp", "dp"))
    out_specs = (P("expert", "fsdp", "dp"), P("expert", "fsdp", "dp"))
    return jax.shard_map(
        on_device, mesh=mesh, in_specs=in_specs, out_specs=out_specs, check_vma=False
    )
```

```python
import functools
import math

import jax
import jax.numpy as jnp
from jax import lax
from jax.experimental import pallas as pl
from jax.experimental.pallas import tpu as pltpu
from jax.sharding import PartitionSpec as P

ROWS = 768
COLS = 2048
MATS = 6
RB = 192
CB = 512
RING = 8
PLANE = 16
COUNT = 96 * ROWS * COLS
SUB = 4
CW = CB // SUB
KW = 2 * CW
STEP = 64
WINDOW = 2
GB = 256
NB = ROWS // GB
OWNER = (0, 1, 2, 4, 5, 6)
DETOUR = {3: 3, 0: 7}
ORDER = (2, 5, 1, 4, 0, 3)

COEF_A = 3.4445
COEF_B = -4.775
COEF_C = 2.0315
DECAY = 0.95
FACTOR = 0.2 * math.sqrt(max(ROWS, COLS))

f32 = jnp.float32
bf16 = jnp.bfloat16


def kernel(
    g_hbm, m_hbm, dir_hbm, nm_hbm,
    g_own, grec, psend, prec, summed, mom, nest, x0, x1, y, g_part, g_send, g_recv, gram, poly, via, col_sq, plane_sq,
    own_sem, mom_sem, cs_sem, cr_sem, rs_sem, rr_sem, sq_send, sq_recv,
    ns_sem, xr_sem, xl_sem, gs_sem, gr_sem, ds_sem, dr_sem, dl_sem, nm_sem, vs_sem, vr_sem,
):
    dp = lax.axis_index("dp")
    expert = lax.axis_index("expert")
    zl = lax.axis_index("fsdp")
    zh = dp // 2
    core = lax.rem(dp, 2)
    z = zh * 4 + zl
    other = 1 - core
    odd = lax.rem(expert, 2)
    partner = expert + 1 - 2 * odd
    place = lax.rem(z + RING - 2 * odd, RING)

    def at(zz, cc):
        zz = lax.rem(zz, RING)
        return {"dp": (zz // 4) * 2 + cc, "fsdp": lax.rem(zz, 4)}

    def across_x(zz):
        return {"expert": partner, **at(zz, core)}

    def owner_of(i):
        return at(2 * odd + OWNER[i], core)

    def remote(src, dst, send, recv, device):
        return pltpu.make_async_remote_copy(
            src_ref=src, dst_ref=dst, send_sem=send, recv_sem=recv, device_id=device
        )

    def block(index):
        return pl.ds(pl.multiple_of(index * CB, CB), CB)

    far = (1 - zh) * 2
    near = zh * 2
    own = []
    for i in range(MATS):
        own.append(pltpu.make_async_copy(g_hbm.at[0, i], g_own.at[i], own_sem.at[i]))
    for copy in own:
        copy.start()
    load_mom = pltpu.make_async_copy(m_hbm, mom, mom_sem)
    load_mom.start()

    barrier = pltpu.get_barrier_semaphore()
    for step in range(1, RING):
        for cc in (core, other):
            pl.semaphore_signal(barrier, inc=1, device_id=at(z + step, cc))
    pl.semaphore_signal(barrier, inc=1, device_id=at(z, other))
    for step in range(1, PLANE):
        pl.semaphore_signal(barrier, inc=1, device_id={"expert": lax.rem(expert + step, PLANE)})
    for copy in own:
        copy.wait()
    pl.semaphore_wait(barrier, 2 * RING - 1 + PLANE - 1)

    swap = []
    for half, first in ((0, far), (1, near)):
        for i in range(MATS):
            n = half * MATS + i
            swap.append(remote(
                g_own.at[i, :, block(first + other)], grec.at[half, i], cs_sem.at[n], cr_sem.at[n], at(z, other)
            ))
    swap[0].start()
    swap[1].start()

    def each(rows, step, work, init=0):
        return lax.fori_loop(
            0, rows // step, lambda t, carry: work(pl.ds(pl.multiple_of(t * step, step), step), carry), init
        )

    across = []
    for i in range(MATS):
        swap[i].wait_recv()
        if i + 2 < MATS:
            swap[i + 2].start()

        def add_far(rows, carry):
            psend[i, rows, :] = (g_own[i, rows, block(far + core)].astype(f32) + grec[0, i, rows, :].astype(f32)).astype(bf16)
            return carry

        each(RB, STEP, add_far)
        if i >= WINDOW:
            across[i - WINDOW].wait_send()
        copy = remote(psend.at[i], prec.at[i], rs_sem.at[i], rr_sem.at[i], at(z + 4, core))
        copy.start()
        across.append(copy)
        if i + 2 == MATS:
            for copy in swap[MATS:]:
                copy.start()
    for i in range(MATS):
        swap[MATS + i].wait_recv()

        def add_near(rows, carry):
            summed[i, rows, :] = g_own[i, rows, block(near + core)].astype(f32) + grec[1, i, rows, :].astype(f32)
            return carry

        each(RB, STEP, add_near)
    for copy in swap:
        copy.wait_send()

    total = jnp.zeros((STEP, 128), f32)
    for i in range(MATS):
        across[i].wait_recv()

        def add_across(rows, carry):
            s = summed[i, rows, :] + prec[i, rows, :].astype(f32)
            summed[i, rows, :] = s
            q = s * s
            return carry + ((q[:, 0:128] + q[:, 128:256]) + (q[:, 256:384] + q[:, 384:512]))

        total = each(RB, STEP, add_across, total)
    total = sum(total[8 * t : 8 * t + 8] for t in range(STEP // 8))

    mine = z * 2 + core
    col_sq[mine] = total
    for step in range(1, RING):
        for cc in (core, other):
            remote(col_sq.at[mine], col_sq.at[mine], sq_send.at[0], sq_recv.at[0], at(z + step, cc)).start()
    remote(col_sq.at[mine], col_sq.at[mine], sq_send.at[0], sq_recv.at[0], at(z, other)).start()
    all_col = remote(
        col_sq.at[pl.ds(0, 2 * RING - 1)], col_sq.at[pl.ds(0, 2 * RING - 1)], sq_send.at[0], sq_recv.at[0], at(z, other)
    )
    all_col.wait_recv()
    plane_sq[expert] = jnp.sum(col_sq[...], axis=0)
    for step in range(1, PLANE):
        remote(
            plane_sq.at[expert], plane_sq.at[expert], sq_send.at[1], sq_recv.at[1],
            {"expert": lax.rem(expert + step, PLANE)},
        ).start()
    all_plane = remote(
        plane_sq.at[pl.ds(0, PLANE - 1)], plane_sq.at[pl.ds(0, PLANE - 1)], sq_send.at[1], sq_recv.at[1], at(z, other)
    )
    for copy in across[MATS - WINDOW :]:
        copy.wait_send()
    load_mom.wait()
    all_plane.wait_recv()
    total_sq = jnp.sum(jnp.sum(plane_sq[...], axis=0), axis=(0, 1), keepdims=True)
    clip = jnp.minimum(f32(1.0), 1.0 / jnp.sqrt(total_sq / f32(COUNT) + 1e-06))

    row_at = pl.ds(pl.multiple_of(zl * RB, RB), RB)
    half_at = pl.ds(pl.multiple_of(zh * CW, CW), CW)
    store_nm = []
    for i in ORDER:

        def momentum_step(rows, carry):
            s = clip * summed[i, rows, :]
            m = DECAY * mom[i, rows, :] + s
            mom[i, rows, :] = m
            nest[i, rows, :] = (s + DECAY * m).astype(bf16)
            return carry

        each(RB, STEP, momentum_step)

        direct = place != OWNER[i]
        if i in DETOUR:
            direct = jnp.logical_and(direct, place != DETOUR[i])

        @pl.when(direct)
        def _():
            for k in range(SUB):
                remote(
                    nest.at[i, :, pl.ds(k * CW, CW)], x0.at[k, row_at, half_at], ns_sem.at[i], xr_sem.at[k], owner_of(i)
                ).start()

        @pl.when(place == OWNER[i])
        def _():
            for k in range(SUB):
                pltpu.make_async_copy(
                    nest.at[i, :, pl.ds(k * CW, CW)], x0.at[k, row_at, half_at], xl_sem.at[k]
                ).start()

        if i in DETOUR:

            @pl.when(place == DETOUR[i])
            def _():
                for k in range(SUB):
                    remote(
                        nest.at[i, :, pl.ds(k * CW, CW)], via.at[k], ns_sem.at[i], vr_sem.at[k], across_x(z)
                    ).start()

        copy = pltpu.make_async_copy(mom.at[i], nm_hbm.at[i], nm_sem.at[i])
        copy.start()
        store_nm.append(copy)

    @pl.when(lax.rem(place, 4) == 1)
    def _():
        for k in range(SUB):
            remote(via.at[k], via.at[k], vs_sem.at[k], vr_sem.at[k], across_x(z)).wait_recv()
            remote(via.at[k], x0.at[k, row_at, half_at], vs_sem.at[k], xr_sem.at[k], across_x(z + 1)).start()

    mat = place - place // 4
    is_owner = lax.rem(place, 4) != 3

    def nt_dot(a, b):
        return lax.dot_general(a, b, (((1,), (1,)), ((), ())), preferred_element_type=f32)

    def nn_dot(a, b):
        return lax.dot_general(a, b, (((1,), (0,)), ((), ())), preferred_element_type=f32)

    def swap_gram(sweep, b):
        there = (pl.ds(b * GB, GB), pl.ds(0, (b + 1) * GB))
        g_send[sweep, *there] = g_part[there].astype(bf16)
        copy = remote(
            g_send.at[sweep, *there], g_recv.at[sweep, *there], gs_sem.at[sweep, b], gr_sem.at[sweep, b], at(z, other)
        )
        copy.start()
        return copy

    def fill_gram(sweep, scale):
        for b in range(NB):
            rows = pl.ds(b * GB, GB)
            for a in range(b + 1):
                cols = pl.ds(a * GB, GB)
                v = g_part[rows, cols] + g_recv[sweep, rows, cols].astype(f32)
                v = (v if scale is None else (v * scale) * scale).astype(bf16)
                gram[rows, cols] = v
                if a < b:
                    gram[cols, rows] = v.T

    def make_poly():
        for b in range(NB):
            rows = pl.ds(b * GB, GB)
            g = gram[rows, :]
            poly[rows, :] = (COEF_B * g.astype(f32) + COEF_C * nn_dot(g, gram[...])).astype(bf16)

    @pl.when(is_owner)
    def _():
        for k in range(SUB):
            pltpu.make_async_copy(nest.at[0, :, pl.ds(0, CW)], x0.at[k, row_at, half_at], xl_sem.at[k]).wait()
            seven = x0.at[k, pl.ds(0, (RING - 1) * RB // 2), :]
            remote(seven, seven, xr_sem.at[k], xr_sem.at[k], at(z, other)).wait_recv()
            swaps = []
            for b in reversed(range(NB)):
                rows, cols = pl.ds(b * GB, GB), pl.ds(0, (b + 1) * GB)
                v = nt_dot(x0[k, rows, :], x0[k, cols, :])
                g_part[rows, cols] = v if k == 0 else g_part[rows, cols] + v
                if k == SUB - 1:
                    swaps.append(swap_gram(0, b))
        for copy in swaps:
            copy.wait()

        diag = jnp.zeros((128, 128), f32)
        eye = lax.broadcasted_iota(jnp.int32, (128, 128), 0) == lax.broadcasted_iota(jnp.int32, (128, 128), 1)
        for b in range(ROWS // 128):
            s = pl.ds(b * 128, 128)
            diag = diag + jnp.where(eye, g_part[s, s] + g_recv[0, s, s].astype(f32), 0.0)
        norm = jnp.sqrt(jnp.sum(diag, axis=(0, 1), keepdims=True))
        inv = 1.0 / (norm + 1e-07)
        fill_gram(0, inv)
        make_poly()
        for k in range(SUB):
            for b in range(NB):
                rows = pl.ds(b * GB, GB)
                v = COEF_A * x0[k, rows, :].astype(f32) + nn_dot(poly[rows, :], x0[k])
                x1[k, rows, :] = (v * inv).astype(bf16)
        swaps = []
        for b in reversed(range(NB)):
            rows, cols = pl.ds(b * GB, GB), pl.ds(0, (b + 1) * GB)
            v = nt_dot(x1[0, rows, :], x1[0, cols, :])
            for k in range(1, SUB):
                v = v + nt_dot(x1[k, rows, :], x1[k, cols, :])
            g_part[rows, cols] = v
            swaps.append(swap_gram(1, b))
        for copy in swaps:
            copy.wait()
        fill_gram(1, None)
        make_poly()
        for k in range(SUB):
            for b in range(NB):
                rows = pl.ds(b * GB, GB)
                v = COEF_A * x1[k, rows, :].astype(f32) + nn_dot(poly[rows, :], x1[k])
                y[k, rows, :] = (FACTOR * v).astype(bf16)
            part = pl.ds(k * CW, CW)

            def tile_of(there):
                rows = pl.ds(pl.multiple_of(lax.rem(there, 4) * RB, RB), RB)
                return y.at[k, rows, pl.ds(pl.multiple_of((there // 4) * CW, CW), CW)]

            def send_direct(step):
                there = lax.rem(z + step, RING)
                remote(
                    tile_of(there), dir_hbm.at[mat, :, part], ds_sem.at[k], dr_sem.at[mat], at(there, core)
                ).start()

            for step in (4, 3, 5, 2, 6, 1, 7):
                send_direct(step)
            pltpu.make_async_copy(y.at[k, row_at, half_at], dir_hbm.at[mat, :, part], dl_sem.at[k]).start()

    @pl.when(lax.rem(place, 4) == 1)
    def _():
        for k in range(SUB):
            remote(via.at[k], via.at[k], vs_sem.at[k], vr_sem.at[k], across_x(z)).wait_send()

    for i in range(MATS):

        @pl.when(place != OWNER[i])
        def _():
            done = remote(nest.at[i], dir_hbm.at[i], ns_sem.at[i], dr_sem.at[i], at(z, other))
            done.wait_send()
            done.wait_recv()

    @pl.when(is_owner)
    def _():
        for k in range(SUB):
            seven = y.at[k, pl.ds(0, (RING - 1) * RB // 2), :]
            remote(seven, seven, ds_sem.at[k], dr_sem.at[0], at(z, other)).wait_send()
            pltpu.make_async_copy(y.at[k, row_at, half_at], dir_hbm.at[mat, :, pl.ds(k * CW, CW)], dl_sem.at[k]).wait()

    all_col.wait_send()
    all_plane.wait_send()
    for copy in store_nm:
        copy.wait()


def on_device(grads, momentum):
    vmem = pltpu.VMEM
    dma = pltpu.SemaphoreType.DMA
    return pl.pallas_call(
        kernel,
        out_shape=(
            jax.ShapeDtypeStruct((MATS, RB, CB), bf16),
            jax.ShapeDtypeStruct((MATS, RB, CB), f32),
        ),
        in_specs=[pl.BlockSpec(memory_space=pl.ANY)] * 2,
        out_specs=(pl.BlockSpec(memory_space=pl.ANY),) * 2,
        scratch_shapes=[
            vmem((MATS, RB, COLS), bf16),
            vmem((2, MATS, RB, CB), bf16),
            vmem((MATS, RB, CB), bf16),
            vmem((MATS, RB, CB), bf16),
            vmem((MATS, RB, CB), f32),
            vmem((MATS, RB, CB), f32),
            vmem((MATS, RB, CB), bf16),
            vmem((SUB, ROWS, KW), bf16),
            vmem((SUB, ROWS, KW), bf16),
            vmem((SUB, ROWS, KW), bf16),
            vmem((ROWS, ROWS), f32),
            vmem((2, ROWS, ROWS), bf16),
            vmem((2, ROWS, ROWS), bf16),
            vmem((ROWS, ROWS), bf16),
            vmem((ROWS, ROWS), bf16),
            vmem((SUB, RB, CW), bf16),
            vmem((2 * RING, 8, 128), f32),
            vmem((PLANE, 8, 128), f32),
            dma((MATS,)),
            dma,
            dma((2 * MATS,)),
            dma((2 * MATS,)),
            dma((MATS,)),
            dma((MATS,)),
            dma((2,)),
            dma((2,)),
            dma((MATS,)),
            dma((SUB,)),
            dma((SUB,)),
            dma((2, NB)),
            dma((2, NB)),
            dma((SUB,)),
            dma((MATS,)),
            dma((SUB,)),
            dma((MATS,)),
            dma((SUB,)),
            dma((SUB,)),
        ],
        compiler_params=pltpu.CompilerParams(
            collective_id=0, has_side_effects=True, vmem_limit_bytes=56 * 2**20
        ),
        cost_estimate=pl.CostEstimate(flops=7 * 10**9, bytes_accessed=12 * 10**6, transcendentals=0),
    )(grads, momentum)


def solution(mesh):
    in_specs = (P("dp", "expert", "fsdp", None), P("expert", "fsdp", "dp"))
    out_specs = (P("expert", "fsdp", "dp"), P("expert", "fsdp", "dp"))
    return jax.shard_map(
        on_device, mesh=mesh, in_specs=in_specs, out_specs=out_specs, check_vma=False
    )
```

```python
import functools
import math

import jax
import jax.numpy as jnp
from jax import lax
from jax.experimental import pallas as pl
from jax.experimental.pallas import tpu as pltpu
from jax.sharding import PartitionSpec as P

ROWS = 768
COLS = 2048
MATS = 6
RB = 192
CB = 512
RING = 8
PLANE = 16
COUNT = 96 * ROWS * COLS
SUB = 4
CW = CB // SUB
KW = 2 * CW
STEP = 64
WINDOW = 2
GB = 256
NB = ROWS // GB
OWNER = (0, 1, 2, 4, 5, 6)
DETOUR = {3: 3, 0: 7}
GROUPS = ((2, 5), (1, 4), (0, 3))

COEF_A = 3.4445
COEF_B = -4.775
COEF_C = 2.0315
DECAY = 0.95
FACTOR = 0.2 * math.sqrt(max(ROWS, COLS))

f32 = jnp.float32
bf16 = jnp.bfloat16


def kernel(
    g_hbm, m_hbm, direction, mom,
    g_own, grec, psend, prec, summed, nest, x0, y, g_part, g_send, g_recv, gram, poly, poly2, mix, via, col_sq, plane_sq,
    own_sem, mom_sem, cs_sem, cr_sem, rs_sem, rr_sem, sq_send, sq_recv,
    ns_sem, xr_sem, xl_sem, gs_sem, gr_sem, ds_sem, dr_sem, dl_sem, vs_sem, vr_sem,
):
    dp = lax.axis_index("dp")
    expert = lax.axis_index("expert")
    zl = lax.axis_index("fsdp")
    zh = dp // 2
    core = lax.rem(dp, 2)
    z = zh * 4 + zl
    other = 1 - core
    odd = lax.rem(expert, 2)
    partner = expert + 1 - 2 * odd
    place = lax.rem(z + RING - 2 * odd, RING)

    def at(zz, cc):
        zz = lax.rem(zz, RING)
        return {"dp": (zz // 4) * 2 + cc, "fsdp": lax.rem(zz, 4)}

    def across_x(zz):
        return {"expert": partner, **at(zz, core)}

    def owner_of(i):
        return at(2 * odd + OWNER[i], core)

    def remote(src, dst, send, recv, device):
        return pltpu.make_async_remote_copy(
            src_ref=src, dst_ref=dst, send_sem=send, recv_sem=recv, device_id=device
        )

    def block(index):
        return pl.ds(pl.multiple_of(index * CB, CB), CB)

    far = (1 - zh) * 2
    near = zh * 2
    own = []
    for i in range(MATS):
        own.append(pltpu.make_async_copy(g_hbm.at[0, i], g_own.at[i], own_sem.at[i]))
    for copy in own:
        copy.start()
    load_mom = pltpu.make_async_copy(m_hbm, mom, mom_sem)
    load_mom.start()

    barrier = pltpu.get_barrier_semaphore()
    for step in range(1, RING):
        for cc in (core, other):
            pl.semaphore_signal(barrier, inc=1, device_id=at(z + step, cc))
    pl.semaphore_signal(barrier, inc=1, device_id=at(z, other))
    for step in range(1, PLANE):
        pl.semaphore_signal(barrier, inc=1, device_id={"expert": lax.rem(expert + step, PLANE)})
    for copy in own:
        copy.wait()
    pl.semaphore_wait(barrier, 2 * RING - 1 + PLANE - 1)

    swap = []
    for half, first in ((0, far), (1, near)):
        for i in range(MATS):
            n = half * MATS + i
            swap.append(remote(
                g_own.at[i, :, block(first + other)], grec.at[half, i], cs_sem.at[n], cr_sem.at[n], at(z, other)
            ))
    swap[0].start()
    swap[1].start()

    def each(rows, step, work, init=0):
        return lax.fori_loop(
            0, rows // step, lambda t, carry: work(pl.ds(pl.multiple_of(t * step, step), step), carry), init
        )

    across = []
    for i in range(MATS):
        swap[i].wait_recv()
        if i + 2 < MATS:
            swap[i + 2].start()

        def add_far(rows, carry):
            psend[i, rows, :] = (g_own[i, rows, block(far + core)].astype(f32) + grec[0, i, rows, :].astype(f32)).astype(bf16)
            return carry

        each(RB, STEP, add_far)
        if i >= WINDOW:
            across[i - WINDOW].wait_send()
        copy = remote(psend.at[i], prec.at[i], rs_sem.at[i], rr_sem.at[i], at(z + 4, core))
        copy.start()
        across.append(copy)
        if i + 2 == MATS:
            for copy in swap[MATS:]:
                copy.start()
    for i in range(MATS):
        swap[MATS + i].wait_recv()

        def add_near(rows, carry):
            summed[i, rows, :] = g_own[i, rows, block(near + core)].astype(f32) + grec[1, i, rows, :].astype(f32)
            return carry

        each(RB, STEP, add_near)
    for copy in swap:
        copy.wait_send()

    total = jnp.zeros((STEP, 128), f32)
    for i in range(MATS):
        across[i].wait_recv()

        def add_across(rows, carry):
            s = summed[i, rows, :] + prec[i, rows, :].astype(f32)
            summed[i, rows, :] = s
            q = s * s
            return carry + ((q[:, 0:128] + q[:, 128:256]) + (q[:, 256:384] + q[:, 384:512]))

        total = each(RB, STEP, add_across, total)
    total = sum(total[8 * t : 8 * t + 8] for t in range(STEP // 8))

    mine = z * 2 + core
    col_sq[mine] = total
    for step in range(1, RING):
        for cc in (core, other):
            remote(col_sq.at[mine], col_sq.at[mine], sq_send.at[0], sq_recv.at[0], at(z + step, cc)).start()
    remote(col_sq.at[mine], col_sq.at[mine], sq_send.at[0], sq_recv.at[0], at(z, other)).start()
    all_col = remote(
        col_sq.at[pl.ds(0, 2 * RING - 1)], col_sq.at[pl.ds(0, 2 * RING - 1)], sq_send.at[0], sq_recv.at[0], at(z, other)
    )
    all_col.wait_recv()
    plane_sq[expert] = jnp.sum(col_sq[...], axis=0)
    for step in range(1, PLANE):
        remote(
            plane_sq.at[expert], plane_sq.at[expert], sq_send.at[1], sq_recv.at[1],
            {"expert": lax.rem(expert + step, PLANE)},
        ).start()
    all_plane = remote(
        plane_sq.at[pl.ds(0, PLANE - 1)], plane_sq.at[pl.ds(0, PLANE - 1)], sq_send.at[1], sq_recv.at[1], at(z, other)
    )
    for copy in across[MATS - WINDOW :]:
        copy.wait_send()
    load_mom.wait()
    all_plane.wait_recv()
    total_sq = jnp.sum(jnp.sum(plane_sq[...], axis=0), axis=(0, 1), keepdims=True)
    clip = jnp.minimum(f32(1.0), 1.0 / jnp.sqrt(total_sq / f32(COUNT) + 1e-06))

    row_at = pl.ds(pl.multiple_of(zl * RB, RB), RB)
    half_at = pl.ds(pl.multiple_of(zh * CW, CW), CW)
    def step_tile(i):
        def momentum_step(rows, carry):
            s = clip * summed[i, rows, :]
            m = DECAY * mom[i, rows, :] + s
            mom[i, rows, :] = m
            nest[i, rows, :] = (s + DECAY * m).astype(bf16)
            return carry

        each(RB, STEP, momentum_step)

    def send_part(i, k):
        direct = place != OWNER[i]
        if i in DETOUR:
            direct = jnp.logical_and(direct, place != DETOUR[i])
        part = nest.at[i, :, pl.ds(k * CW, CW)]

        @pl.when(direct)
        def _():
            remote(part, x0.at[k, row_at, half_at], ns_sem.at[i], xr_sem.at[k], owner_of(i)).start()

        @pl.when(place == OWNER[i])
        def _():
            pltpu.make_async_copy(part, x0.at[k, row_at, half_at], xl_sem.at[k]).start()

        if i in DETOUR:

            @pl.when(place == DETOUR[i])
            def _():
                remote(part, via.at[k], ns_sem.at[i], vr_sem.at[k], across_x(z)).start()

    for group in GROUPS:
        for i in group:
            step_tile(i)
        for k in range(SUB):
            for i in group:
                send_part(i, k)

    @pl.when(lax.rem(place, 4) == 1)
    def _():
        for k in range(SUB):
            remote(via.at[k], via.at[k], vs_sem.at[k], vr_sem.at[k], across_x(z)).wait_recv()
            remote(via.at[k], x0.at[k, row_at, half_at], vs_sem.at[k], xr_sem.at[k], across_x(z + 1)).start()

    mat = place - place // 4
    is_owner = lax.rem(place, 4) != 3

    def nt_dot(a, b):
        return lax.dot_general(a, b, (((1,), (1,)), ((), ())), preferred_element_type=f32)

    def nn_dot(a, b):
        return lax.dot_general(a, b, (((1,), (0,)), ((), ())), preferred_element_type=f32)

    def lower(b):
        return pl.ds(b * GB, GB), pl.ds(0, (b + 1) * GB)

    def put(ref, b, value):
        rows, cols = lower(b)
        value = value.astype(bf16)
        ref[rows, cols] = value
        for a in range(b):
            ref[pl.ds(a * GB, GB), rows] = value[:, a * GB : (a + 1) * GB].T

    def swap_gram(b):
        there = lower(b)
        g_send[there] = g_part[there].astype(bf16)
        copy = remote(g_send.at[there], g_recv.at[there], gs_sem.at[b], gr_sem.at[b], at(z, other))
        copy.start()
        return copy

    def make_poly(ref):
        for b in range(NB):
            rows, cols = lower(b)
            square = nn_dot(gram[rows, :], gram[:, cols])
            put(ref, b, COEF_B * gram[rows, cols].astype(f32) + COEF_C * square)

    @pl.when(is_owner)
    def _():
        for k in range(SUB):
            pltpu.make_async_copy(nest.at[0, :, pl.ds(0, CW)], x0.at[k, row_at, half_at], xl_sem.at[k]).wait()
            seven = x0.at[k, pl.ds(0, (RING - 1) * RB // 2), :]
            remote(seven, seven, xr_sem.at[k], xr_sem.at[k], at(z, other)).wait_recv()
            swaps = []
            for b in reversed(range(NB)):
                rows, cols = lower(b)
                v = nt_dot(x0[k, rows, :], x0[k, cols, :])
                g_part[rows, cols] = v if k == 0 else g_part[rows, cols] + v
                if k == SUB - 1:
                    swaps.append(swap_gram(b))
        for copy in swaps:
            copy.wait()

        diag = jnp.zeros((128, 128), f32)
        eye = lax.broadcasted_iota(jnp.int32, (128, 128), 0) == lax.broadcasted_iota(jnp.int32, (128, 128), 1)
        for b in range(ROWS // 128):
            s = pl.ds(b * 128, 128)
            diag = diag + jnp.where(eye, g_part[s, s] + g_recv[s, s].astype(f32), 0.0)
        norm = jnp.sqrt(jnp.sum(diag, axis=(0, 1), keepdims=True))
        inv = 1.0 / (norm + 1e-07)
        for b in range(NB):
            there = lower(b)
            put(gram, b, ((g_part[there] + g_recv[there].astype(f32)) * inv) * inv)
        make_poly(poly)
        for b in range(NB):
            rows, cols = lower(b)
            v = COEF_A * gram[rows, cols].astype(f32) + nn_dot(poly[rows, :], gram[:, cols])
            g_part[rows, cols] = v
            put(mix, b, v)
        for b in range(NB):
            rows, cols = lower(b)
            put(gram, b, COEF_A * g_part[rows, cols] + nn_dot(mix[rows, :], poly[:, cols]))
        make_poly(poly2)
        own_row = []
        for b in range(NB):
            rows, cols = lower(b)
            v = COEF_A * (poly[rows, cols].astype(f32) + poly2[rows, cols].astype(f32))
            v = v + nn_dot(poly2[rows, :], poly[:, cols])
            on_diag = lax.broadcasted_iota(jnp.int32, v.shape, 1) == b * GB + lax.broadcasted_iota(jnp.int32, v.shape, 0)
            own_row.append(COEF_A * COEF_A + jnp.sum(jnp.where(on_diag, v, 0.0), axis=1, keepdims=True))
            put(mix, b, jnp.where(on_diag, 0.0, v))
        scale = FACTOR * inv
        for k in range(SUB):
            for b in range(NB):
                rows = pl.ds(b * GB, GB)
                v = own_row[b] * x0[k, rows, :].astype(f32) + nn_dot(mix[rows, :], x0[k])
                y[k, rows, :] = (v * scale).astype(bf16)
            part = pl.ds(k * CW, CW)

            def tile_of(there):
                rows = pl.ds(pl.multiple_of(lax.rem(there, 4) * RB, RB), RB)
                return y.at[k, rows, pl.ds(pl.multiple_of((there // 4) * CW, CW), CW)]

            def send_direct(step):
                there = lax.rem(z + step, RING)
                remote(
                    tile_of(there), direction.at[mat, :, part], ds_sem.at[k], dr_sem.at[mat], at(there, core)
                ).start()

            for step in (4, 3, 5, 2, 6, 1, 7):
                send_direct(step)
            pltpu.make_async_copy(y.at[k, row_at, half_at], direction.at[mat, :, part], dl_sem.at[k]).start()

    @pl.when(lax.rem(place, 4) == 1)
    def _():
        for k in range(SUB):
            remote(via.at[k], via.at[k], vs_sem.at[k], vr_sem.at[k], across_x(z)).wait_send()

    for i in range(MATS):

        @pl.when(place != OWNER[i])
        def _():
            done = remote(nest.at[i], direction.at[i], ns_sem.at[i], dr_sem.at[i], at(z, other))
            done.wait_send()
            done.wait_recv()

    @pl.when(is_owner)
    def _():
        for k in range(SUB):
            seven = y.at[k, pl.ds(0, (RING - 1) * RB // 2), :]
            remote(seven, seven, ds_sem.at[k], dr_sem.at[0], at(z, other)).wait_send()
            pltpu.make_async_copy(y.at[k, row_at, half_at], direction.at[mat, :, pl.ds(k * CW, CW)], dl_sem.at[k]).wait()

    all_col.wait_send()
    all_plane.wait_send()


def on_device(grads, momentum):
    vmem = pltpu.VMEM
    dma = pltpu.SemaphoreType.DMA
    return pl.pallas_call(
        kernel,
        out_shape=(
            vmem((MATS, RB, CB), bf16),
            vmem((MATS, RB, CB), f32),
        ),
        in_specs=[pl.BlockSpec(memory_space=pl.ANY)] * 2,
        out_specs=(pl.BlockSpec(memory_space=vmem),) * 2,
        scratch_shapes=[
            vmem((MATS, RB, COLS), bf16),
            vmem((2, MATS, RB, CB), bf16),
            vmem((MATS, RB, CB), bf16),
            vmem((MATS, RB, CB), bf16),
            vmem((MATS, RB, CB), f32),
            vmem((MATS, RB, CB), bf16),
            vmem((SUB, ROWS, KW), bf16),
            vmem((SUB, ROWS, KW), bf16),
            vmem((ROWS, ROWS), f32),
            vmem((ROWS, ROWS), bf16),
            vmem((ROWS, ROWS), bf16),
            vmem((ROWS, ROWS), bf16),
            vmem((ROWS, ROWS), bf16),
            vmem((ROWS, ROWS), bf16),
            vmem((ROWS, ROWS), bf16),
            vmem((SUB, RB, CW), bf16),
            vmem((2 * RING, 8, 128), f32),
            vmem((PLANE, 8, 128), f32),
            dma((MATS,)),
            dma,
            dma((2 * MATS,)),
            dma((2 * MATS,)),
            dma((MATS,)),
            dma((MATS,)),
            dma((2,)),
            dma((2,)),
            dma((MATS,)),
            dma((SUB,)),
            dma((SUB,)),
            dma((NB,)),
            dma((NB,)),
            dma((SUB,)),
            dma((MATS,)),
            dma((SUB,)),
            dma((SUB,)),
            dma((SUB,)),
        ],
        compiler_params=pltpu.CompilerParams(
            collective_id=0, has_side_effects=True, vmem_limit_bytes=58 * 2**20
        ),
        cost_estimate=pl.CostEstimate(flops=7 * 10**9, bytes_accessed=12 * 10**6, transcendentals=0),
    )(grads, momentum)


def solution(mesh):
    in_specs = (P("dp", "expert", "fsdp", None), P("expert", "fsdp", "dp"))
    out_specs = (P("expert", "fsdp", "dp"), P("expert", "fsdp", "dp"))
    return jax.shard_map(
        on_device, mesh=mesh, in_specs=in_specs, out_specs=out_specs, check_vma=False
    )
```

```python
import math

import jax
import jax.numpy as jnp
from jax import lax
from jax.experimental import pallas as pl
from jax.experimental.pallas import tpu as pltpu
from jax.sharding import PartitionSpec as P

ROWS = 768
COLS = 2048
MATS = 6
RB = 192
CB = 512
RING = 8
PLANE = 16
COUNT = 96 * ROWS * COLS
SUB = 4
CW = CB // SUB
KW = 2 * CW
STEP = 64
WINDOW = 2
GB = 256
NB = ROWS // GB
FAR_FIRST = (4, 3, 5, 2, 6, 1, 7)
OWNER = (0, 1, 2, 4, 5, 6)
DETOUR = {3: 3, 0: 7}
GROUPS = ((2, 5), (1, 4), (0, 3))

COEF_A = 3.4445
COEF_B = -4.775
COEF_C = 2.0315
DECAY = 0.95
FACTOR = 0.2 * math.sqrt(max(ROWS, COLS))

f32 = jnp.float32
bf16 = jnp.bfloat16


def kernel(
    g_hbm, m_hbm, direction, mom,
    g_own, grec, psend, prec, summed, nest, x0, y, g_part, g_send, g_recv, gram, poly, poly2, mix, via, col_sq, plane_sq,
    own_sem, mom_sem, cs_sem, cr_sem, rs_sem, rr_sem, sq_send, sq_recv,
    ns_sem, xr_sem, xl_sem, gs_sem, gr_sem, ds_sem, dr_sem, dl_sem, vs_sem, vr_sem,
):
    dp = lax.axis_index("dp")
    expert = lax.axis_index("expert")
    zl = lax.axis_index("fsdp")
    zh = dp // 2
    core = lax.rem(dp, 2)
    z = zh * 4 + zl
    other = 1 - core
    odd = lax.rem(expert, 2)
    partner = expert + 1 - 2 * odd
    place = lax.rem(z + RING - 2 * odd, RING)

    def at(zz, cc):
        zz = lax.rem(zz, RING)
        return {"dp": (zz // 4) * 2 + cc, "fsdp": lax.rem(zz, 4)}

    def across_x(zz):
        return {"expert": partner, **at(zz, core)}

    def owner_of(i):
        return at(2 * odd + OWNER[i], core)

    def remote(src, dst, send, recv, device):
        return pltpu.make_async_remote_copy(
            src_ref=src, dst_ref=dst, send_sem=send, recv_sem=recv, device_id=device
        )

    def block(index):
        return pl.ds(pl.multiple_of(index * CB, CB), CB)

    far = (1 - zh) * 2
    near = zh * 2
    own = []
    for i in range(MATS):
        own.append(pltpu.make_async_copy(g_hbm.at[0, i], g_own.at[i], own_sem.at[i]))
    for copy in own:
        copy.start()
    load_mom = pltpu.make_async_copy(m_hbm, mom, mom_sem)
    load_mom.start()

    barrier = pltpu.get_barrier_semaphore()
    for step in FAR_FIRST:
        for cc in (core, other):
            pl.semaphore_signal(barrier, inc=1, device_id=at(z + step, cc))
    pl.semaphore_signal(barrier, inc=1, device_id=at(z, other))
    for step in range(1, PLANE):
        pl.semaphore_signal(barrier, inc=1, device_id={"expert": lax.rem(expert + step, PLANE)})
    for copy in own:
        copy.wait()
    pl.semaphore_wait(barrier, 2 * RING - 1 + PLANE - 1)

    swap = []
    for half, first in ((0, far), (1, near)):
        for i in range(MATS):
            n = half * MATS + i
            swap.append(remote(
                g_own.at[i, :, block(first + other)], grec.at[half, i], cs_sem.at[n], cr_sem.at[n], at(z, other)
            ))
    swap[0].start()
    swap[1].start()

    def each(rows, step, work, init=0):
        return lax.fori_loop(
            0, rows // step, lambda t, carry: work(pl.ds(pl.multiple_of(t * step, step), step), carry), init
        )

    across = []
    for i in range(MATS):
        swap[i].wait_recv()
        if i + 2 < MATS:
            swap[i + 2].start()

        def add_far(rows, carry):
            psend[i, rows, :] = (g_own[i, rows, block(far + core)].astype(f32) + grec[0, i, rows, :].astype(f32)).astype(bf16)
            return carry

        each(RB, STEP, add_far)
        if i >= WINDOW:
            across[i - WINDOW].wait_send()
        copy = remote(psend.at[i], prec.at[i], rs_sem.at[i], rr_sem.at[i], at(z + 4, core))
        copy.start()
        across.append(copy)
        if i + 2 == MATS:
            for copy in swap[MATS:]:
                copy.start()
    for i in range(MATS):
        swap[MATS + i].wait_recv()

        def add_near(rows, carry):
            summed[i, rows, :] = g_own[i, rows, block(near + core)].astype(f32) + grec[1, i, rows, :].astype(f32)
            return carry

        each(RB, STEP, add_near)
    for copy in swap:
        copy.wait_send()

    total = jnp.zeros((STEP, 128), f32)
    for i in range(MATS):
        across[i].wait_recv()

        def add_across(rows, carry):
            s = summed[i, rows, :] + prec[i, rows, :].astype(f32)
            summed[i, rows, :] = s
            q = s * s
            return carry + ((q[:, 0:128] + q[:, 128:256]) + (q[:, 256:384] + q[:, 384:512]))

        total = each(RB, STEP, add_across, total)
    total = jnp.sum(total, axis=0, keepdims=True)

    mine = z * 2 + core
    col_sq[mine] = total
    for step in FAR_FIRST:
        for cc in (core, other):
            remote(col_sq.at[mine], col_sq.at[mine], sq_send.at[0], sq_recv.at[0], at(z + step, cc)).start()
    remote(col_sq.at[mine], col_sq.at[mine], sq_send.at[0], sq_recv.at[0], at(z, other)).start()
    all_col = remote(
        col_sq.at[pl.ds(0, 2 * RING - 1)], col_sq.at[pl.ds(0, 2 * RING - 1)], sq_send.at[0], sq_recv.at[0], at(z, other)
    )
    all_col.wait_recv()
    plane_sq[expert] = jnp.sum(col_sq[...], axis=0)
    for dy in (2, 1, 3, 0):
        for dx in (2, 1, 3, 0):
            if dx or dy:
                there = lax.rem(expert // 4 + dy, 4) * 4 + lax.rem(expert + dx, 4)
                remote(
                    plane_sq.at[expert], plane_sq.at[expert], sq_send.at[1], sq_recv.at[1], {"expert": there}
                ).start()
    all_plane = remote(
        plane_sq.at[pl.ds(0, PLANE - 1)], plane_sq.at[pl.ds(0, PLANE - 1)], sq_send.at[1], sq_recv.at[1], at(z, other)
    )
    for copy in across[MATS - WINDOW :]:
        copy.wait_send()
    load_mom.wait()
    all_plane.wait_recv()
    total_sq = jnp.sum(jnp.sum(plane_sq[...], axis=0), axis=(0, 1), keepdims=True)
    clip = jnp.minimum(f32(1.0), 1.0 / jnp.sqrt(total_sq / f32(COUNT) + 1e-06))

    row_at = pl.ds(pl.multiple_of(zl * RB, RB), RB)
    half_at = pl.ds(pl.multiple_of(zh * CW, CW), CW)
    def step_tile(i):
        def momentum_step(rows, carry):
            s = clip * summed[i, rows, :]
            m = DECAY * mom[i, rows, :] + s
            mom[i, rows, :] = m
            nest[i, rows, :] = (s + DECAY * m).astype(bf16)
            return carry

        each(RB, STEP, momentum_step)

    def send_part(i, k):
        direct = place != OWNER[i]
        if i in DETOUR:
            direct = jnp.logical_and(direct, place != DETOUR[i])
        part = nest.at[i, :, pl.ds(k * CW, CW)]

        @pl.when(direct)
        def _():
            remote(part, x0.at[k, row_at, half_at], ns_sem.at[i], xr_sem.at[k], owner_of(i)).start()

        @pl.when(place == OWNER[i])
        def _():
            pltpu.make_async_copy(part, x0.at[k, row_at, half_at], xl_sem.at[k]).start()

        if i in DETOUR:

            @pl.when(place == DETOUR[i])
            def _():
                remote(part, via.at[k], ns_sem.at[i], vr_sem.at[k], across_x(z)).start()

    for group in GROUPS:
        for i in group:
            step_tile(i)
        for k in range(SUB):
            for i in group:
                send_part(i, k)

    @pl.when(lax.rem(place, 4) == 1)
    def _():
        for k in range(SUB):
            remote(via.at[k], via.at[k], vs_sem.at[k], vr_sem.at[k], across_x(z)).wait_recv()
            remote(via.at[k], x0.at[k, row_at, half_at], vs_sem.at[k], xr_sem.at[k], across_x(z + 1)).start()

    mat = place - place // 4
    is_owner = lax.rem(place, 4) != 3

    def nt_dot(a, b):
        return lax.dot_general(a, b, (((1,), (1,)), ((), ())), preferred_element_type=f32)

    def nn_dot(a, b):
        return lax.dot_general(a, b, (((1,), (0,)), ((), ())), preferred_element_type=f32)

    def lower(b):
        return pl.ds(b * GB, GB), pl.ds(0, (b + 1) * GB)

    def put(ref, b, value):
        rows, cols = lower(b)
        value = value.astype(bf16)
        ref[rows, cols] = value
        for a in range(b):
            ref[pl.ds(a * GB, GB), rows] = value[:, a * GB : (a + 1) * GB].T

    def swap_gram(b):
        there = lower(b)
        g_send[there] = g_part[there].astype(bf16)
        copy = remote(g_send.at[there], g_recv.at[there], gs_sem.at[b], gr_sem.at[b], at(z, other))
        copy.start()
        return copy

    def make_poly(ref):
        for b in range(NB):
            rows, cols = lower(b)
            square = nn_dot(gram[rows, :], gram[:, cols])
            put(ref, b, COEF_B * gram[rows, cols].astype(f32) + COEF_C * square)

    @pl.when(is_owner)
    def _():
        for k in range(SUB):
            pltpu.make_async_copy(nest.at[0, :, pl.ds(0, CW)], x0.at[k, row_at, half_at], xl_sem.at[k]).wait()
            seven = x0.at[k, pl.ds(0, (RING - 1) * RB // 2), :]
            remote(seven, seven, xr_sem.at[k], xr_sem.at[k], at(z, other)).wait_recv()
            swaps = []
            for b in reversed(range(NB)):
                rows, cols = lower(b)
                v = nt_dot(x0[k, rows, :], x0[k, cols, :])
                g_part[rows, cols] = v if k == 0 else g_part[rows, cols] + v
                if k == SUB - 1:
                    swaps.append(swap_gram(b))
        for copy in swaps:
            copy.wait()

        diag = jnp.zeros((128, 128), f32)
        eye = lax.broadcasted_iota(jnp.int32, (128, 128), 0) == lax.broadcasted_iota(jnp.int32, (128, 128), 1)
        for b in range(ROWS // 128):
            s = pl.ds(b * 128, 128)
            diag = diag + jnp.where(eye, g_part[s, s] + g_recv[s, s].astype(f32), 0.0)
        norm = jnp.sqrt(jnp.sum(diag, axis=(0, 1), keepdims=True))
        inv = 1.0 / (norm + 1e-07)
        for b in range(NB):
            there = lower(b)
            put(gram, b, ((g_part[there] + g_recv[there].astype(f32)) * inv) * inv)
        make_poly(poly)
        for b in range(NB):
            rows, cols = lower(b)
            v = COEF_A * gram[rows, cols].astype(f32) + nn_dot(poly[rows, :], gram[:, cols])
            g_part[rows, cols] = v
            put(mix, b, v)
        for b in range(NB):
            rows, cols = lower(b)
            put(gram, b, COEF_A * g_part[rows, cols] + nn_dot(mix[rows, :], poly[:, cols]))
        make_poly(poly2)
        own_row = []
        for b in range(NB):
            rows, cols = lower(b)
            v = COEF_A * (poly[rows, cols].astype(f32) + poly2[rows, cols].astype(f32))
            v = v + nn_dot(poly2[rows, :], poly[:, cols])
            on_diag = lax.broadcasted_iota(jnp.int32, v.shape, 1) == b * GB + lax.broadcasted_iota(jnp.int32, v.shape, 0)
            own_row.append(COEF_A * COEF_A + jnp.sum(jnp.where(on_diag, v, 0.0), axis=1, keepdims=True))
            put(mix, b, jnp.where(on_diag, 0.0, v))
        scale = FACTOR * inv
        for k in range(SUB):
            for b in range(NB):
                rows = pl.ds(b * GB, GB)
                v = own_row[b] * x0[k, rows, :].astype(f32) + nn_dot(mix[rows, :], x0[k])
                y[k, rows, :] = (v * scale).astype(bf16)
            part = pl.ds(k * CW, CW)

            def tile_of(there):
                rows = pl.ds(pl.multiple_of(lax.rem(there, 4) * RB, RB), RB)
                return y.at[k, rows, pl.ds(pl.multiple_of((there // 4) * CW, CW), CW)]

            def send_direct(step):
                there = lax.rem(z + step, RING)
                remote(
                    tile_of(there), direction.at[mat, :, part], ds_sem.at[k], dr_sem.at[mat], at(there, core)
                ).start()

            for step in FAR_FIRST:
                send_direct(step)
            pltpu.make_async_copy(y.at[k, row_at, half_at], direction.at[mat, :, part], dl_sem.at[k]).start()

    @pl.when(lax.rem(place, 4) == 1)
    def _():
        for k in range(SUB):
            remote(via.at[k], via.at[k], vs_sem.at[k], vr_sem.at[k], across_x(z)).wait_send()

    for i in range(MATS):

        @pl.when(place != OWNER[i])
        def _():
            done = remote(nest.at[i], direction.at[i], ns_sem.at[i], dr_sem.at[i], at(z, other))
            done.wait_send()
            done.wait_recv()

    @pl.when(is_owner)
    def _():
        for k in range(SUB):
            seven = y.at[k, pl.ds(0, (RING - 1) * RB // 2), :]
            remote(seven, seven, ds_sem.at[k], dr_sem.at[0], at(z, other)).wait_send()
            pltpu.make_async_copy(y.at[k, row_at, half_at], direction.at[mat, :, pl.ds(k * CW, CW)], dl_sem.at[k]).wait()

    all_col.wait_send()
    all_plane.wait_send()


def on_device(grads, momentum):
    vmem = pltpu.VMEM
    dma = pltpu.SemaphoreType.DMA
    return pl.pallas_call(
        kernel,
        out_shape=(
            vmem((MATS, RB, CB), bf16),
            vmem((MATS, RB, CB), f32),
        ),
        in_specs=[pl.BlockSpec(memory_space=pl.ANY)] * 2,
        out_specs=(pl.BlockSpec(memory_space=vmem),) * 2,
        scratch_shapes=[
            vmem((MATS, RB, COLS), bf16),
            vmem((2, MATS, RB, CB), bf16),
            vmem((MATS, RB, CB), bf16),
            vmem((MATS, RB, CB), bf16),
            vmem((MATS, RB, CB), f32),
            vmem((MATS, RB, CB), bf16),
            vmem((SUB, ROWS, KW), bf16),
            vmem((SUB, ROWS, KW), bf16),
            vmem((ROWS, ROWS), f32),
            vmem((ROWS, ROWS), bf16),
            vmem((ROWS, ROWS), bf16),
            vmem((ROWS, ROWS), bf16),
            vmem((ROWS, ROWS), bf16),
            vmem((ROWS, ROWS), bf16),
            vmem((ROWS, ROWS), bf16),
            vmem((SUB, RB, CW), bf16),
            vmem((2 * RING, 1, 128), f32),
            vmem((PLANE, 1, 128), f32),
            dma((MATS,)),
            dma,
            dma((2 * MATS,)),
            dma((2 * MATS,)),
            dma((MATS,)),
            dma((MATS,)),
            dma((2,)),
            dma((2,)),
            dma((MATS,)),
            dma((SUB,)),
            dma((SUB,)),
            dma((NB,)),
            dma((NB,)),
            dma((SUB,)),
            dma((MATS,)),
            dma((SUB,)),
            dma((SUB,)),
            dma((SUB,)),
        ],
        compiler_params=pltpu.CompilerParams(
            collective_id=0, has_side_effects=True, vmem_limit_bytes=58 * 2**20
        ),
        cost_estimate=pl.CostEstimate(flops=7 * 10**9, bytes_accessed=12 * 10**6, transcendentals=0),
    )(grads, momentum)


def solution(mesh):
    in_specs = (P("dp", "expert", "fsdp", None), P("expert", "fsdp", "dp"))
    out_specs = (P("expert", "fsdp", "dp"), P("expert", "fsdp", "dp"))
    return jax.shard_map(
        on_device, mesh=mesh, in_specs=in_specs, out_specs=out_specs, check_vma=False
    )
```

```python
import math

import jax
import jax.numpy as jnp
from jax import lax
from jax.experimental import pallas as pl
from jax.experimental.pallas import tpu as pltpu
from jax.sharding import PartitionSpec as P

ROWS = 768
COLS = 2048
MATS = 6
RB = 192
CB = 512
RING = 8
PLANE = 16
COUNT = 96 * ROWS * COLS
SUB = 4
CW = CB // SUB
KW = 2 * CW
STEP = 64
WINDOW = 2
GB = 256
NB = ROWS // GB
FAR_FIRST = (4, 3, 5, 2, 6, 1, 7)
OWNER = (0, 1, 2, 4, 5, 6)
DETOUR = {3: 3, 0: 7}
GROUPS = ((2,), (5,), (1, 4), (0, 3))

COEF_A = 3.4445
COEF_B = -4.775
COEF_C = 2.0315
DECAY = 0.95
FACTOR = 0.2 * math.sqrt(max(ROWS, COLS))

f32 = jnp.float32
bf16 = jnp.bfloat16


def kernel(
    g_hbm, m_hbm, direction, mom,
    g_own, grec, psend, prec, summed, nest, x0, y, g_part, g_send, g_recv, gram, poly, poly2, mix, via, col_sq, plane_sq,
    own_sem, mom_sem, cs_sem, cr_sem, rs_sem, rr_sem, sq_send, sq_recv,
    ns_sem, xr_sem, xl_sem, gs_sem, gr_sem, ds_sem, dr_sem, dl_sem, vs_sem, vr_sem,
):
    dp = lax.axis_index("dp")
    expert = lax.axis_index("expert")
    zl = lax.axis_index("fsdp")
    zh = dp // 2
    core = lax.rem(dp, 2)
    z = zh * 4 + zl
    other = 1 - core
    odd = lax.rem(expert, 2)
    partner = expert + 1 - 2 * odd
    place = lax.rem(z + RING - 2 * odd, RING)

    def at(zz, cc):
        zz = lax.rem(zz, RING)
        return {"dp": (zz // 4) * 2 + cc, "fsdp": lax.rem(zz, 4)}

    def across_x(zz):
        return {"expert": partner, **at(zz, core)}

    def owner_of(i):
        return at(2 * odd + OWNER[i], core)

    def remote(src, dst, send, recv, device):
        return pltpu.make_async_remote_copy(
            src_ref=src, dst_ref=dst, send_sem=send, recv_sem=recv, device_id=device
        )

    def block(index):
        return pl.ds(pl.multiple_of(index * CB, CB), CB)

    far = (1 - zh) * 2
    near = zh * 2
    own = []
    for i in range(MATS):
        own.append(pltpu.make_async_copy(g_hbm.at[0, i], g_own.at[i], own_sem.at[i]))
    for copy in own:
        copy.start()
    load_mom = pltpu.make_async_copy(m_hbm, mom, mom_sem)
    load_mom.start()

    barrier = pltpu.get_barrier_semaphore()
    for step in FAR_FIRST:
        for cc in (core, other):
            pl.semaphore_signal(barrier, inc=1, device_id=at(z + step, cc))
    pl.semaphore_signal(barrier, inc=1, device_id=at(z, other))
    for step in range(1, PLANE):
        pl.semaphore_signal(barrier, inc=1, device_id={"expert": lax.rem(expert + step, PLANE)})
    for copy in own:
        copy.wait()
    pl.semaphore_wait(barrier, 2 * RING - 1 + PLANE - 1)

    swap = []
    for half, first in ((0, far), (1, near)):
        for i in range(MATS):
            n = half * MATS + i
            swap.append(remote(
                g_own.at[i, :, block(first + other)], grec.at[half, i], cs_sem.at[n], cr_sem.at[n], at(z, other)
            ))
    swap[0].start()
    swap[1].start()

    def each(rows, step, work, init=0):
        return lax.fori_loop(
            0, rows // step, lambda t, carry: work(pl.ds(pl.multiple_of(t * step, step), step), carry), init
        )

    across = []
    for i in range(MATS):
        swap[i].wait_recv()
        if i + 2 < MATS:
            swap[i + 2].start()

        def add_far(rows, carry):
            psend[i, rows, :] = (g_own[i, rows, block(far + core)].astype(f32) + grec[0, i, rows, :].astype(f32)).astype(bf16)
            return carry

        each(RB, STEP, add_far)
        if i >= WINDOW:
            across[i - WINDOW].wait_send()
        copy = remote(psend.at[i], prec.at[i], rs_sem.at[i], rr_sem.at[i], at(z + 4, core))
        copy.start()
        across.append(copy)
        if i + 2 == MATS:
            for copy in swap[MATS:]:
                copy.start()
    for i in range(MATS):
        swap[MATS + i].wait_recv()

        def add_near(rows, carry):
            summed[i, rows, :] = g_own[i, rows, block(near + core)].astype(f32) + grec[1, i, rows, :].astype(f32)
            return carry

        each(RB, STEP, add_near)
    for copy in swap:
        copy.wait_send()

    total = jnp.zeros((STEP, 128), f32)
    for i in range(MATS):
        across[i].wait_recv()

        def add_across(rows, carry):
            s = summed[i, rows, :] + prec[i, rows, :].astype(f32)
            summed[i, rows, :] = s
            q = s * s
            return carry + ((q[:, 0:128] + q[:, 128:256]) + (q[:, 256:384] + q[:, 384:512]))

        total = each(RB, STEP, add_across, total)
    total = jnp.sum(total, axis=0, keepdims=True)

    mine = z * 2 + core
    col_sq[mine] = total
    for step in FAR_FIRST:
        for cc in (core, other):
            remote(col_sq.at[mine], col_sq.at[mine], sq_send.at[0], sq_recv.at[0], at(z + step, cc)).start()
    remote(col_sq.at[mine], col_sq.at[mine], sq_send.at[0], sq_recv.at[0], at(z, other)).start()
    all_col = remote(
        col_sq.at[pl.ds(0, 2 * RING - 1)], col_sq.at[pl.ds(0, 2 * RING - 1)], sq_send.at[0], sq_recv.at[0], at(z, other)
    )
    all_col.wait_recv()
    plane_sq[expert] = jnp.sum(col_sq[...], axis=0)
    for dy in (2, 1, 3, 0):
        for dx in (2, 1, 3, 0):
            if dx or dy:
                there = lax.rem(expert // 4 + dy, 4) * 4 + lax.rem(expert + dx, 4)
                remote(
                    plane_sq.at[expert], plane_sq.at[expert], sq_send.at[1], sq_recv.at[1], {"expert": there}
                ).start()
    all_plane = remote(
        plane_sq.at[pl.ds(0, PLANE - 1)], plane_sq.at[pl.ds(0, PLANE - 1)], sq_send.at[1], sq_recv.at[1], at(z, other)
    )
    for copy in across[MATS - WINDOW :]:
        copy.wait_send()
    load_mom.wait()
    all_plane.wait_recv()
    total_sq = jnp.sum(jnp.sum(plane_sq[...], axis=0), axis=(0, 1), keepdims=True)
    clip = jnp.minimum(f32(1.0), 1.0 / jnp.sqrt(total_sq / f32(COUNT) + 1e-06))

    row_at = pl.ds(pl.multiple_of(zl * RB, RB), RB)
    half_at = pl.ds(pl.multiple_of(zh * CW, CW), CW)
    def step_tile(i):
        def momentum_step(rows, carry):
            s = clip * summed[i, rows, :]
            m = DECAY * mom[i, rows, :] + s
            mom[i, rows, :] = m
            nest[i, rows, :] = (s + DECAY * m).astype(bf16)
            return carry

        each(RB, STEP, momentum_step)

    def send_part(i, k):
        direct = place != OWNER[i]
        if i in DETOUR:
            direct = jnp.logical_and(direct, place != DETOUR[i])
        part = nest.at[i, :, pl.ds(k * CW, CW)]

        @pl.when(direct)
        def _():
            remote(part, x0.at[k, row_at, half_at], ns_sem.at[i], xr_sem.at[k], owner_of(i)).start()

        @pl.when(place == OWNER[i])
        def _():
            pltpu.make_async_copy(part, x0.at[k, row_at, half_at], xl_sem.at[k]).start()

        if i in DETOUR:

            @pl.when(place == DETOUR[i])
            def _():
                remote(part, via.at[k], ns_sem.at[i], vr_sem.at[k], across_x(z)).start()

    for group in GROUPS:
        for i in group:
            step_tile(i)
        for k in range(SUB):
            for i in group:
                send_part(i, k)

    @pl.when(lax.rem(place, 4) == 1)
    def _():
        for k in range(SUB):
            remote(via.at[k], via.at[k], vs_sem.at[k], vr_sem.at[k], across_x(z)).wait_recv()
            remote(via.at[k], x0.at[k, row_at, half_at], vs_sem.at[k], xr_sem.at[k], across_x(z + 1)).start()

    mat = place - place // 4
    is_owner = lax.rem(place, 4) != 3

    def nt_dot(a, b):
        return lax.dot_general(a, b, (((1,), (1,)), ((), ())), preferred_element_type=f32)

    def nn_dot(a, b):
        return lax.dot_general(a, b, (((1,), (0,)), ((), ())), preferred_element_type=f32)

    def lower(b):
        return pl.ds(b * GB, GB), pl.ds(0, (b + 1) * GB)

    def put(ref, b, value):
        rows, cols = lower(b)
        value = value.astype(bf16)
        ref[rows, cols] = value
        for a in range(b):
            ref[pl.ds(a * GB, GB), rows] = value[:, a * GB : (a + 1) * GB].T

    def swap_gram(b):
        there = lower(b)
        g_send[there] = g_part[there].astype(bf16)
        copy = remote(g_send.at[there], g_recv.at[there], gs_sem.at[b], gr_sem.at[b], at(z, other))
        copy.start()
        return copy

    def make_poly(ref):
        for b in range(NB):
            rows, cols = lower(b)
            square = nn_dot(gram[rows, :], gram[:, cols])
            put(ref, b, COEF_B * gram[rows, cols].astype(f32) + COEF_C * square)

    @pl.when(is_owner)
    def _():
        for k in range(SUB):
            pltpu.make_async_copy(nest.at[0, :, pl.ds(0, CW)], x0.at[k, row_at, half_at], xl_sem.at[k]).wait()
            seven = x0.at[k, pl.ds(0, (RING - 1) * RB // 2), :]
            remote(seven, seven, xr_sem.at[k], xr_sem.at[k], at(z, other)).wait_recv()
            swaps = []
            for b in reversed(range(NB)):
                rows, cols = lower(b)
                v = nt_dot(x0[k, rows, :], x0[k, cols, :])
                g_part[rows, cols] = v if k == 0 else g_part[rows, cols] + v
                if k == SUB - 1:
                    swaps.append(swap_gram(b))
        for copy in swaps:
            copy.wait()

        diag = jnp.zeros((128, 128), f32)
        eye = lax.broadcasted_iota(jnp.int32, (128, 128), 0) == lax.broadcasted_iota(jnp.int32, (128, 128), 1)
        for b in range(ROWS // 128):
            s = pl.ds(b * 128, 128)
            diag = diag + jnp.where(eye, g_part[s, s] + g_recv[s, s].astype(f32), 0.0)
        norm = jnp.sqrt(jnp.sum(diag, axis=(0, 1), keepdims=True))
        inv = 1.0 / (norm + 1e-07)
        for b in range(NB):
            there = lower(b)
            put(gram, b, ((g_part[there] + g_recv[there].astype(f32)) * inv) * inv)
        make_poly(poly)
        for b in range(NB):
            rows, cols = lower(b)
            v = COEF_A * gram[rows, cols].astype(f32) + nn_dot(poly[rows, :], gram[:, cols])
            g_part[rows, cols] = v
            put(mix, b, v)
        for b in range(NB):
            rows, cols = lower(b)
            put(gram, b, COEF_A * g_part[rows, cols] + nn_dot(mix[rows, :], poly[:, cols]))
        make_poly(poly2)
        own_row = []
        for b in range(NB):
            rows, cols = lower(b)
            v = COEF_A * (poly[rows, cols].astype(f32) + poly2[rows, cols].astype(f32))
            v = v + nn_dot(poly2[rows, :], poly[:, cols])
            on_diag = lax.broadcasted_iota(jnp.int32, v.shape, 1) == b * GB + lax.broadcasted_iota(jnp.int32, v.shape, 0)
            own_row.append(COEF_A * COEF_A + jnp.sum(jnp.where(on_diag, v, 0.0), axis=1, keepdims=True))
            put(mix, b, jnp.where(on_diag, 0.0, v))
        scale = FACTOR * inv
        for k in range(SUB):
            for b in range(NB):
                rows = pl.ds(b * GB, GB)
                v = own_row[b] * x0[k, rows, :].astype(f32) + nn_dot(mix[rows, :], x0[k])
                y[k, rows, :] = (v * scale).astype(bf16)
            part = pl.ds(k * CW, CW)

            def tile_of(there):
                rows = pl.ds(pl.multiple_of(lax.rem(there, 4) * RB, RB), RB)
                return y.at[k, rows, pl.ds(pl.multiple_of((there // 4) * CW, CW), CW)]

            def send_direct(step):
                there = lax.rem(z + step, RING)
                remote(
                    tile_of(there), direction.at[mat, :, part], ds_sem.at[k], dr_sem.at[mat], at(there, core)
                ).start()

            for step in FAR_FIRST:
                send_direct(step)
            pltpu.make_async_copy(y.at[k, row_at, half_at], direction.at[mat, :, part], dl_sem.at[k]).start()

    @pl.when(lax.rem(place, 4) == 1)
    def _():
        for k in range(SUB):
            remote(via.at[k], via.at[k], vs_sem.at[k], vr_sem.at[k], across_x(z)).wait_send()

    for i in range(MATS):

        @pl.when(place != OWNER[i])
        def _():
            done = remote(nest.at[i], direction.at[i], ns_sem.at[i], dr_sem.at[i], at(z, other))
            done.wait_send()
            done.wait_recv()

    @pl.when(is_owner)
    def _():
        for k in range(SUB):
            seven = y.at[k, pl.ds(0, (RING - 1) * RB // 2), :]
            remote(seven, seven, ds_sem.at[k], dr_sem.at[0], at(z, other)).wait_send()
            pltpu.make_async_copy(y.at[k, row_at, half_at], direction.at[mat, :, pl.ds(k * CW, CW)], dl_sem.at[k]).wait()

    all_col.wait_send()
    all_plane.wait_send()


def hand_on(d_in, n_in, d_out, n_out, sem):
    copies = []
    for i in range(MATS):
        copies.append(pltpu.make_async_copy(n_in.at[i], n_out.at[i], sem.at[0, i]))
        copies.append(pltpu.make_async_copy(d_in.at[i], d_out.at[i], sem.at[1, i]))
    for copy in copies:
        copy.start()
    for copy in copies:
        copy.wait()


def on_device(grads, momentum):
    results = whole_step(grads, momentum)
    return pl.pallas_call(
        hand_on,
        out_shape=(
            jax.ShapeDtypeStruct((MATS, RB, CB), bf16),
            jax.ShapeDtypeStruct((MATS, RB, CB), f32),
        ),
        in_specs=[pl.BlockSpec(memory_space=pltpu.VMEM)] * 2,
        out_specs=(pl.BlockSpec(memory_space=pl.ANY),) * 2,
        scratch_shapes=[pltpu.SemaphoreType.DMA((2, MATS))],
        compiler_params=pltpu.CompilerParams(vmem_limit_bytes=4 * 2**20),
    )(*results)


def whole_step(grads, momentum):
    vmem = pltpu.VMEM
    dma = pltpu.SemaphoreType.DMA
    return pl.pallas_call(
        kernel,
        out_shape=(
            vmem((MATS, RB, CB), bf16),
            vmem((MATS, RB, CB), f32),
        ),
        in_specs=[pl.BlockSpec(memory_space=pl.ANY)] * 2,
        out_specs=(pl.BlockSpec(memory_space=vmem),) * 2,
        scratch_shapes=[
            vmem((MATS, RB, COLS), bf16),
            vmem((2, MATS, RB, CB), bf16),
            vmem((MATS, RB, CB), bf16),
            vmem((MATS, RB, CB), bf16),
            vmem((MATS, RB, CB), f32),
            vmem((MATS, RB, CB), bf16),
            vmem((SUB, ROWS, KW), bf16),
            vmem((SUB, ROWS, KW), bf16),
            vmem((ROWS, ROWS), f32),
            vmem((ROWS, ROWS), bf16),
            vmem((ROWS, ROWS), bf16),
            vmem((ROWS, ROWS), bf16),
            vmem((ROWS, ROWS), bf16),
            vmem((ROWS, ROWS), bf16),
            vmem((ROWS, ROWS), bf16),
            vmem((SUB, RB, CW), bf16),
            vmem((2 * RING, 1, 128), f32),
            vmem((PLANE, 1, 128), f32),
            dma((MATS,)),
            dma,
            dma((2 * MATS,)),
            dma((2 * MATS,)),
            dma((MATS,)),
            dma((MATS,)),
            dma((2,)),
            dma((2,)),
            dma((MATS,)),
            dma((SUB,)),
            dma((SUB,)),
            dma((NB,)),
            dma((NB,)),
            dma((SUB,)),
            dma((MATS,)),
            dma((SUB,)),
            dma((SUB,)),
            dma((SUB,)),
        ],
        compiler_params=pltpu.CompilerParams(
            collective_id=0, has_side_effects=True, vmem_limit_bytes=58 * 2**20
        ),
        cost_estimate=pl.CostEstimate(flops=7 * 10**9, bytes_accessed=12 * 10**6, transcendentals=0),
    )(grads, momentum)


def solution(mesh):
    in_specs = (P("dp", "expert", "fsdp", None), P("expert", "fsdp", "dp"))
    out_specs = (P("expert", "fsdp", "dp"), P("expert", "fsdp", "dp"))
    return jax.shard_map(
        on_device, mesh=mesh, in_specs=in_specs, out_specs=out_specs, check_vma=False
    )
```
